128 devices in a mesh: seq: 32 (over x, z, core), chan: 4 (over y).
Axes of the slice: x: 4, y: 4, z: 4, core: 2. Of those that a mesh axis runs over, the one named last changes fastest.
Arguments:
- signal: bfloat16 [16384, 3072], P('seq', 'chan'), may hold values from -6 to 6
- rates: float32 [32, 3072], P(None, 'chan'), may hold values from 0 to 1, as said below
- freqs: float32 [32, 3072], P(None, 'chan'), may hold values from -1 to 1
- coeffs: float32 [2, 32, 3072], P(None, None, 'chan'), may hold values from -1 to 1
- skip: float32 [3072], P('chan'), may hold values from -4 to 4
- weight: bfloat16 [3072, 3072], P('seq', 'chan'), may hold values from -0.109375 to 0.109375
Outputs:
- mixed: bfloat16 [16384, 3072], P('seq', 'chan')
The draws below stay inside these ranges and needn't reach their ends.
Inputs may be any that keep to these rules, and one draw needn't show every extreme that they name: Positive decay rates per position.
All inputs are finite; a program needn't handle non-finite values.
Results may differ from the reference program's by a relative error of at most 0.011.
Values may be sent and summed in bfloat16 or wider, within the bound.
No kernel may reach another device: no remote copies, remote signals or barrier semaphores. Data moves between devices by JAX's collectives and lax.ppermute only.
A program may use at most 128 MiB of HBM per device.

```python
import math
import jax
import jax.numpy as jnp
from jax import lax

H = 3072
NM = 32
TOK_DEV = 512
LENGTH = 16384
N_SEQ = 32


def decay_values(key, slow_share):
    pick_key, slow_key, fast_key = jax.random.split(key, 3)
    slow_mask = jax.random.uniform(pick_key, (NM, H)) < slow_share
    slow_rate = jnp.exp(jax.random.uniform(slow_key, (NM, H), minval=math.log(0.1), maxval=math.log(2.0))) / LENGTH
    fast_rate = jnp.exp(jax.random.uniform(fast_key, (NM, H), minval=math.log(1.0 / 40.0), maxval=math.log(0.25)))
    return jnp.where(slow_mask, slow_rate, fast_rate).astype(jnp.float32)


def draw_rates(key, part):
    share = 0.5
    return decay_values(key, share)


def draw_coeffs(key, part):
    share = 0.5
    decays = decay_values(key, share)
    key = jax.random.fold_in(key, 7)
    memory = jnp.minimum(1.0 / -jnp.expm1(-2.0 * decays), LENGTH / 2.0)
    spread = jnp.sqrt(1.0 / (2.0 * NM * memory))
    normal_values = jnp.clip(jax.random.normal(key, (2, NM, H), jnp.float32), -5.0, 5.0)
    return (normal_values * spread[None]).astype(jnp.float32)


def shard_levels(rng, dims, shards, least, top_value):
    gain, own = 1.0, jax.random.fold_in(rng, 6)
    for position, blocks in shards:
        steps = jnp.exp(jax.random.uniform(jax.random.fold_in(own, position), (blocks,), jnp.float32, least / len(shards), top_value / len(shards)))
        gain = gain * jnp.repeat(steps, dims[position] // blocks).reshape([-1 if axis == position else 1 for axis in range(len(dims))])
    return gain


def gaussian(stream_key, shape, scale, most, pieces=(), kind=jnp.bfloat16):
    factor_of = shard_levels(stream_key, shape, pieces, -0.22, 0.18) if pieces else 1.0
    entries = jax.random.normal(stream_key, shape, jnp.float32) * scale * factor_of
    return jnp.minimum(jnp.maximum(entries, -most), most).astype(kind)


def setup_inputs(seed: int = 0) -> dict:
    streams_of = jax.random.split(jax.random.key(seed), 7)
    signal = gaussian(streams_of[0], (LENGTH, H), 1.0, 6.0, ((0, 32), (1, 4)))
    rates = draw_rates(jax.random.fold_in(streams_of[6], 71), 0)
    freqs = jnp.clip(jax.random.uniform(streams_of[2], (NM, H), jnp.float32, -1.0, 1.0) * shard_levels(streams_of[2], (NM, H), ((1, 4),), -0.4, 0.0), -1.0, 1.0)
    coeffs = draw_coeffs(jax.random.fold_in(streams_of[6], 71), 0)
    skip = gaussian(streams_of[4], (H,), 1.0, 4.0, ((0, 4),), jnp.float32)
    weight = gaussian(streams_of[5], (H, H), H ** -0.5, 0.109375, ((0, 32), (1, 4)))
    return dict(signal=signal, rates=rates, freqs=freqs, coeffs=coeffs, skip=skip, weight=weight)


def reference(signal, rates, freqs, coeffs, skip, weight):
    magnitude = jnp.exp(-rates)
    lam_re = magnitude * jnp.cos(freqs)
    lam_im = magnitude * jnp.sin(freqs)
    coef_re = coeffs[0]
    coef_im = coeffs[1]

    def advance(carry, row):
        state_re, state_im = carry
        values = row.astype(jnp.float32)
        next_re = lam_re * state_re - lam_im * state_im + values[None, :]
        next_im = lam_re * state_im + lam_im * state_re
        output = 2.0 * jnp.sum(coef_re * next_re - coef_im * next_im, axis=0) + skip * values
        return (next_re, next_im), output

    zero_state = jnp.zeros(rates.shape, jnp.float32)
    _, conv = lax.scan(advance, (zero_state, zero_state), signal)
    act = jax.nn.gelu(conv).astype(jnp.bfloat16)
    act_blocks = act.reshape(N_SEQ, TOK_DEV, H)

    def project(block_rows):
        return jnp.dot(block_rows, weight, preferred_element_type=jnp.float32)

    proj = lax.map(project, act_blocks).reshape(LENGTH, H)
    return (signal.astype(jnp.float32) + proj).astype(jnp.bfloat16)
```

```python
import jax
import jax.numpy as jnp
from jax import lax
from jax.experimental import pallas as pl
from jax.experimental.pallas import tpu as pltpu
from jax.sharding import PartitionSpec as P

BLK = 32
LANES = 128
GROUP = 4

f32 = jnp.float32
bf16 = jnp.bfloat16


def cmul(ar, ai, br, bi):
    return ar * br - ai * bi, ar * bi + ai * br


def decay(rates_ref, freqs_ref):
    size = jnp.exp(-rates_ref[...])
    angle = freqs_ref[...]
    return size * jnp.cos(angle), size * jnp.sin(angle)


def ends_kernel(u_ref, r_ref, f_ref, part_ref, end_ref, send_ref, step_ref, whole_ref, uf, table):
    uf[...] = u_ref[...].astype(f32)
    lr, li = decay(r_ref, f_ref)
    powers = [(jnp.ones_like(lr), jnp.zeros_like(lr)), (lr, li)]
    for j in range(2, BLK + 1):
        half = powers[j // 2]
        powers.append(cmul(*half, *powers[j - j // 2]))
    for j in range(BLK):
        table[j, 0] = powers[j][0]
        table[j, 1] = powers[j][1]
    sr, si = powers[BLK]
    step_ref[0] = sr
    step_ref[1] = si
    wr, wi = sr, si
    count = BLK
    while count < u_ref.shape[0]:
        wr, wi = cmul(wr, wi, wr, wi)
        count *= 2
    whole_ref[0] = wr
    whole_ref[1] = wi

    def group(g, end):
        er, ei = end
        accs = [[jnp.zeros_like(lr), jnp.zeros_like(lr)] for _ in range(GROUP)]
        for b in range(BLK):
            tr = table[BLK - 1 - b, 0]
            ti = table[BLK - 1 - b, 1]
            for i in range(GROUP):
                row = uf[pl.ds((g * GROUP + i) * BLK + b, 1), :]
                accs[i][0] += tr * row
                accs[i][1] += ti * row
        for i in range(GROUP):
            part_ref[g * GROUP + i, 0] = accs[i][0]
            part_ref[g * GROUP + i, 1] = accs[i][1]
            er, ei = cmul(er, ei, sr, si)
            er = er + accs[i][0]
            ei = ei + accs[i][1]
        return er, ei

    er, ei = lax.fori_loop(
        0, u_ref.shape[0] // BLK // GROUP, group, (jnp.zeros_like(lr), jnp.zeros_like(lr))
    )
    end_ref[0] = er
    end_ref[1] = ei
    send_ref[0] = er.astype(bf16)
    send_ref[1] = ei.astype(bf16)


def inner_kernel(u_ref, r_ref, f_ref, c_ref, skip_ref, coef_ref, base_ref, pad, rows, taps):
    modes = r_ref.shape[0]
    lr, li = decay(r_ref, f_ref)
    q2 = cmul(lr, li, lr, li)
    q4 = cmul(*q2, *q2)
    q8 = cmul(*q4, *q4)
    cr = 2.0 * c_ref[0]
    ci = 2.0 * c_ref[1]
    first = cmul(cr, ci, lr, li)
    for k, pair in enumerate((first, (lr, li), q2, q4, q8)):
        rows[2 * k] = pair[0]
        rows[2 * k + 1] = pair[1]
    place = lax.broadcasted_iota(jnp.int32, (8, LANES), 0)
    bits = [(place & (1 << k)) != 0 for k in range(3)]

    def mode(n, sums):
        row = [jnp.broadcast_to(rows[k, pl.ds(n, 1), :], (8, LANES)) for k in range(10)]
        vr, vi = row[0], row[1]
        for k in range(3):
            nr, ni = cmul(vr, vi, row[2 + 2 * k], row[3 + 2 * k])
            vr = jnp.where(bits[k], nr, vr)
            vi = jnp.where(bits[k], ni, vi)
        out = []
        for i in range(BLK // 8):
            coef_ref[n, 0, 8 * i : 8 * i + 8] = vr
            coef_ref[n, 1, 8 * i : 8 * i + 8] = -vi
            out.append(sums[i] + vr)
            if i + 1 < BLK // 8:
                vr, vi = cmul(vr, vi, row[8], row[9])
        return tuple(out)

    zero = jnp.zeros((8, LANES), f32)
    sums = lax.fori_loop(0, modes, mode, (zero,) * (BLK // 8), unroll=2)
    taps[0:1] = jnp.sum(cr, axis=0, keepdims=True) + skip_ref[...]
    for i in range(BLK // 8):
        taps[8 * i + 1 : 8 * i + 9] = sums[i]
    blocks = u_ref.shape[0] // BLK
    pad[:, 0:8] = jnp.zeros((blocks, 8, LANES), f32)
    pad[:, 8:] = u_ref[...].astype(f32).reshape(blocks, BLK, LANES)

    def group(g, _):
        accs = [[zero] * (BLK // 8) for _ in range(GROUP)]
        for j in range(BLK):
            tap = jnp.broadcast_to(taps[j : j + 1], (8, LANES))
            for i in range(BLK // 8):
                if 8 * i + 7 >= j:
                    for k in range(GROUP):
                        accs[k][i] += tap * pad[g * GROUP + k, 8 + 8 * i - j : 16 + 8 * i - j]
        for k in range(GROUP):
            for i in range(BLK // 8):
                base_ref[pl.ds((g * GROUP + k) * BLK + 8 * i, 8), :] = accs[k][i]
        return 0

    lax.fori_loop(0, blocks // GROUP, group, 0)


def finish_kernel(part_ref, step_ref, coef_ref, base_ref, own_ref, w_ref, q1_ref, q2_ref, q3_ref, act_ref, held):
    hr = own_ref[0]
    hi = own_ref[1]
    for k, q in enumerate((q1_ref, q2_ref, q3_ref)):
        ar, ai = cmul(w_ref[k, 0], w_ref[k, 1], q[0].astype(f32), q[1].astype(f32))
        hr = hr + ar
        hi = hi + ai
    sr = step_ref[0]
    si = step_ref[1]
    blocks = part_ref.shape[0]
    modes = hr.shape[0]
    for a in range(blocks):
        held[a, 0] = hr
        held[a, 1] = hi
        if a + 1 < blocks:
            hr, hi = cmul(hr, hi, sr, si)
            hr = hr + part_ref[a, 0]
            hi = hi + part_ref[a, 1]
    many = 8

    def group(g, _):
        accs = tuple(base_ref[pl.ds((g * many + k) * BLK, BLK), :] for k in range(many))

        def mode(n, accs):
            cr = coef_ref[n, 0]
            ci = coef_ref[n, 1]
            return tuple(
                accs[k]
                + (
                    cr * held[g * many + k, 0, pl.ds(n, 1), :]
                    + ci * held[g * many + k, 1, pl.ds(n, 1), :]
                )
                for k in range(many)
            )

        accs = lax.fori_loop(0, modes, mode, accs, unroll=4)
        for k in range(many):
            act_ref[pl.ds((g * many + k) * BLK, BLK), :] = jax.nn.gelu(accs[k]).astype(bf16)
        return 0

    lax.fori_loop(0, blocks // many, group, 0)


def params(limit=48):
    return pltpu.CompilerParams(vmem_limit_bytes=limit << 20)


def ends(signal, rates, freqs):
    tokens, channels = signal.shape
    modes = rates.shape[0]
    blocks = tokens // BLK
    pair = pl.BlockSpec((2, modes, LANES), lambda i: (0, 0, i))
    return pl.pallas_call(
        ends_kernel,
        grid=(channels // LANES,),
        in_specs=[
            pl.BlockSpec((tokens, LANES), lambda i: (0, i)),
            pl.BlockSpec((modes, LANES), lambda i: (0, i)),
            pl.BlockSpec((modes, LANES), lambda i: (0, i)),
        ],
        out_specs=[
            pl.BlockSpec((blocks, 2, modes, LANES), lambda i: (0, 0, 0, i)),
            pair,
            pair,
            pair,
            pair,
        ],
        out_shape=[
            jax.ShapeDtypeStruct((blocks, 2, modes, channels), f32),
            jax.ShapeDtypeStruct((2, modes, channels), f32),
            jax.ShapeDtypeStruct((2, modes, channels), bf16),
            jax.ShapeDtypeStruct((2, modes, channels), f32),
            jax.ShapeDtypeStruct((2, modes, channels), f32),
        ],
        scratch_shapes=[
            pltpu.VMEM((tokens, LANES), f32),
            pltpu.VMEM((BLK, 2, modes, LANES), f32),
        ],
        compiler_params=params(),
        cost_estimate=pl.CostEstimate(flops=10**9, bytes_accessed=6 * 10**6, transcendentals=0),
    )(signal, rates, freqs)


def inner(signal, rates, freqs, coeffs, skip):
    tokens, channels = signal.shape
    modes = rates.shape[0]
    blocks = tokens // BLK
    return pl.pallas_call(
        inner_kernel,
        grid=(channels // LANES,),
        in_specs=[
            pl.BlockSpec((tokens, LANES), lambda i: (0, i)),
            pl.BlockSpec((modes, LANES), lambda i: (0, i)),
            pl.BlockSpec((modes, LANES), lambda i: (0, i)),
            pl.BlockSpec((2, modes, LANES), lambda i: (0, 0, i)),
            pl.BlockSpec((1, LANES), lambda i: (0, i)),
        ],
        out_specs=[
            pl.BlockSpec((modes, 2, BLK, LANES), lambda i: (0, 0, 0, i)),
            pl.BlockSpec((tokens, LANES), lambda i: (0, i)),
        ],
        out_shape=[
            jax.ShapeDtypeStruct((modes, 2, BLK, channels), f32),
            jax.ShapeDtypeStruct((tokens, channels), f32),
        ],
        scratch_shapes=[
            pltpu.VMEM((blocks, BLK + 8, LANES), f32),
            pltpu.VMEM((10, modes, LANES), f32),
            pltpu.VMEM((BLK + 8, LANES), f32),
        ],
        compiler_params=params(),
        cost_estimate=pl.CostEstimate(flops=5 * 10**8, bytes_accessed=8 * 10**6, transcendentals=0),
    )(signal, rates, freqs, coeffs, skip.reshape(1, channels))


def finish(first, count, part, step, coef, base, own, weights, arrived):
    blocks, _, modes, _ = part.shape
    tokens = base.shape[0]
    pair = pl.BlockSpec((2, modes, LANES), lambda i: (0, 0, i + first))
    return pl.pallas_call(
        finish_kernel,
        grid=(count,),
        in_specs=[
            pl.BlockSpec((blocks, 2, modes, LANES), lambda i: (0, 0, 0, i + first)),
            pair,
            pl.BlockSpec((modes, 2, BLK, LANES), lambda i: (0, 0, 0, i + first)),
            pl.BlockSpec((tokens, LANES), lambda i: (0, i + first)),
            pair,
            pl.BlockSpec((3, 2, modes, LANES), lambda i: (0, 0, 0, i + first)),
            pair,
            pair,
            pair,
        ],
        out_specs=pl.BlockSpec((tokens, LANES), lambda i: (0, i)),
        out_shape=jax.ShapeDtypeStruct((tokens, count * LANES), bf16),
        scratch_shapes=[pltpu.VMEM((blocks, 2, modes, LANES), f32)],
        compiler_params=params(),
        cost_estimate=pl.CostEstimate(
            flops=10**9 // 6 * count, bytes_accessed=2 * 10**6 * count, transcendentals=0
        ),
    )(part, step, coef, base, own, weights, *arrived)


def times(a, b):
    ar, ai = a[0].astype(f32), a[1].astype(f32)
    br, bi = b[0].astype(f32), b[1].astype(f32)
    return jnp.stack([ar * br - ai * bi, ar * bi + ai * br])


def local(signal, rates, freqs, coeffs, skip, weight):
    wide = lax.all_gather(weight, "seq", axis=0, tiled=True)
    part, end, send, step, whole = ends(signal, rates, freqs)

    index = lax.axis_index("seq")
    x, z, c = index // 8, index // 2 % 4, index % 2
    core = [(i, i ^ 1) for i in range(32)]

    def along_z(k):
        return [(i, i // 8 * 8 + (i // 2 + k) % 4 * 2 + i % 2) for i in range(32)]

    def along_x(k):
        return [(i, (i + 8 * k) % 32) for i in range(32)]

    other = lax.ppermute(send, "seq", core).astype(f32)
    lower = jnp.where(c == 0, end, other)
    upper = jnp.where(c == 0, other, end)
    chip = (times(whole, lower) + upper).astype(bf16)

    unit = jnp.stack([jnp.ones_like(rates), jnp.zeros_like(rates)])
    p1 = times(whole, whole)
    p2 = times(p1, p1)
    p3 = times(p2, p1)
    p4 = times(p2, p2)
    p8 = times(p4, p4)
    chips = [unit, p1, p2, p3]

    def pick(k):
        return jnp.where(k == 0, unit, jnp.where(k == 1, p1, jnp.where(k == 2, p2, p3)))

    mine = jnp.where(c == 0, unit, whole)

    from_z = [lax.ppermute(chip, "seq", along_z(k)) for k in (1, 2, 3)]
    line = times(pick(3 - z), chip)
    for k in (1, 2, 3):
        line = line + times(pick(3 - (z - k) % 4), from_z[k - 1])
    line = line.astype(bf16)
    own = jnp.zeros_like(end)
    for k in (1, 2, 3):
        own = own + jnp.where(z >= k, times(chips[k - 1], from_z[k - 1]), 0.0)
    own = times(mine, own) + jnp.where(c == 1, lower, 0.0)

    from_x = [lax.ppermute(line, "seq", along_x(k)) for k in (1, 2, 3)]
    here = times(mine, pick(z))
    weights = jnp.stack(
        [
            jnp.where(x >= k, times(here, far), 0.0)
            for k, far in ((1, unit), (2, p4), (3, p8))
        ]
    )
    coef, base = inner(signal, rates, freqs, coeffs, skip)

    slabs = 2
    count = signal.shape[1] // LANES // slabs
    ring = lambda k: [(i, (i + k) % 4) for i in range(4)]
    half = signal.shape[0] // 2
    y = lax.axis_index("chan")
    width = count * LANES
    pieces = []
    for s in range(slabs):
        act = finish(s * count, count, part, step, coef, base, own, weights, from_x)
        up = lax.ppermute(act, "chan", ring(1))
        down = lax.ppermute(act, "chan", ring(3))
        far_up = lax.ppermute(up[:half], "chan", ring(1))
        far_down = lax.ppermute(down[half:], "chan", ring(3))
        pieces.append((act, up, down, jnp.concatenate([far_up, far_down])))
    total = signal.astype(f32)
    for k, off in enumerate((0, 3, 1, 2)):
        for s in range(slabs):
            rows = lax.dynamic_slice_in_dim(
                wide, (y + off) % 4 * signal.shape[1] + s * width, width, 0
            )
            total = total + jnp.dot(pieces[s][k], rows, preferred_element_type=f32)
    return total.astype(bf16)


def solution(mesh):
    in_specs = (
        P("seq", "chan"),
        P(None, "chan"),
        P(None, "chan"),
        P(None, None, "chan"),
        P("chan"),
        P("seq", "chan"),
    )
    return jax.shard_map(
        local, mesh=mesh, in_specs=in_specs, out_specs=P("seq", "chan"), check_vma=False
    )
```

```python
import jax
import jax.numpy as jnp
from jax import lax
from jax.experimental import pallas as pl
from jax.experimental.pallas import tpu as pltpu
from jax.sharding import PartitionSpec as P

BLK = 32
LANES = 128
GROUP = 4

f32 = jnp.float32
bf16 = jnp.bfloat16


def cmul(ar, ai, br, bi):
    return ar * br - ai * bi, ar * bi + ai * br


def decay(rates_ref, freqs_ref):
    size = jnp.exp(-rates_ref[...])
    angle = freqs_ref[...]
    return size * jnp.cos(angle), size * jnp.sin(angle)


def ends_kernel(u_ref, r_ref, f_ref, part_ref, end_ref, send_ref, step_ref, power_ref, uf, table):
    uf[...] = u_ref[...].astype(f32)
    lr, li = decay(r_ref, f_ref)
    powers = [(jnp.ones_like(lr), jnp.zeros_like(lr)), (lr, li)]
    for j in range(2, BLK + 1):
        half = powers[j // 2]
        powers.append(cmul(*half, *powers[j - j // 2]))
    for j in range(BLK):
        table[j, 0] = powers[j][0]
        table[j, 1] = powers[j][1]
    sr, si = powers[BLK]
    step_ref[0] = sr
    step_ref[1] = si
    wr, wi = sr, si
    count = BLK
    while count < u_ref.shape[0]:
        wr, wi = cmul(wr, wi, wr, wi)
        count *= 2
    for k in range(power_ref.shape[0]):
        power_ref[k, 0] = wr
        power_ref[k, 1] = wi
        wr, wi = cmul(wr, wi, wr, wi)

    def group(g, end):
        er, ei = end
        accs = [[jnp.zeros_like(lr), jnp.zeros_like(lr)] for _ in range(GROUP)]
        for b in range(BLK):
            tr = table[BLK - 1 - b, 0]
            ti = table[BLK - 1 - b, 1]
            for i in range(GROUP):
                row = uf[pl.ds((g * GROUP + i) * BLK + b, 1), :]
                accs[i][0] += tr * row
                accs[i][1] += ti * row
        for i in range(GROUP):
            part_ref[g * GROUP + i, 0] = accs[i][0]
            part_ref[g * GROUP + i, 1] = accs[i][1]
            er, ei = cmul(er, ei, sr, si)
            er = er + accs[i][0]
            ei = ei + accs[i][1]
        return er, ei

    er, ei = lax.fori_loop(
        0, u_ref.shape[0] // BLK // GROUP, group, (jnp.zeros_like(lr), jnp.zeros_like(lr))
    )
    end_ref[0] = er
    end_ref[1] = ei
    send_ref[0] = er.astype(bf16)
    send_ref[1] = ei.astype(bf16)


def inner_kernel(u_ref, r_ref, f_ref, c_ref, skip_ref, coef_ref, base_ref, pad, rows, taps):
    modes = r_ref.shape[0]
    lr, li = decay(r_ref, f_ref)
    q2 = cmul(lr, li, lr, li)
    q4 = cmul(*q2, *q2)
    q8 = cmul(*q4, *q4)
    cr = 2.0 * c_ref[0]
    ci = 2.0 * c_ref[1]
    first = cmul(cr, ci, lr, li)
    for k, pair in enumerate((first, (lr, li), q2, q4, q8)):
        rows[2 * k] = pair[0]
        rows[2 * k + 1] = pair[1]
    place = lax.broadcasted_iota(jnp.int32, (8, LANES), 0)
    bits = [(place & (1 << k)) != 0 for k in range(3)]

    def mode(n, sums):
        row = [jnp.broadcast_to(rows[k, pl.ds(n, 1), :], (8, LANES)) for k in range(10)]
        vr, vi = row[0], row[1]
        for k in range(3):
            nr, ni = cmul(vr, vi, row[2 + 2 * k], row[3 + 2 * k])
            vr = jnp.where(bits[k], nr, vr)
            vi = jnp.where(bits[k], ni, vi)
        out = []
        for i in range(BLK // 8):
            coef_ref[n, 0, 8 * i : 8 * i + 8] = vr
            coef_ref[n, 1, 8 * i : 8 * i + 8] = -vi
            out.append(sums[i] + vr)
            if i + 1 < BLK // 8:
                vr, vi = cmul(vr, vi, row[8], row[9])
        return tuple(out)

    zero = jnp.zeros((8, LANES), f32)
    sums = lax.fori_loop(0, modes, mode, (zero,) * (BLK // 8), unroll=8)
    taps[0:1] = jnp.sum(cr, axis=0, keepdims=True) + skip_ref[...]
    for i in range(BLK // 8):
        taps[8 * i + 1 : 8 * i + 9] = sums[i]
    blocks = u_ref.shape[0] // BLK
    pad[:, 0:8] = jnp.zeros((blocks, 8, LANES), f32)
    pad[:, 8:] = u_ref[...].astype(f32).reshape(blocks, BLK, LANES)

    def group(g, _):
        accs = [[zero] * (BLK // 8) for _ in range(GROUP)]
        for j in range(BLK):
            tap = jnp.broadcast_to(taps[j : j + 1], (8, LANES))
            for i in range(BLK // 8):
                if 8 * i + 7 >= j:
                    for k in range(GROUP):
                        accs[k][i] += tap * pad[g * GROUP + k, 8 + 8 * i - j : 16 + 8 * i - j]
        for k in range(GROUP):
            for i in range(BLK // 8):
                base_ref[pl.ds((g * GROUP + k) * BLK + 8 * i, 8), :] = accs[k][i]
        return 0

    lax.fori_loop(0, blocks // GROUP, group, 0)


def finish_kernel(part_ref, step_ref, coef_ref, base_ref, own_ref, w_ref, q_ref, act_ref, held):
    hr = own_ref[0]
    hi = own_ref[1]
    ar, ai = cmul(w_ref[0], w_ref[1], q_ref[0].astype(f32), q_ref[1].astype(f32))
    hr = hr + ar
    hi = hi + ai
    sr = step_ref[0]
    si = step_ref[1]
    blocks = part_ref.shape[0]
    modes = hr.shape[0]
    for a in range(blocks):
        held[a, 0] = hr
        held[a, 1] = hi
        if a + 1 < blocks:
            hr, hi = cmul(hr, hi, sr, si)
            hr = hr + part_ref[a, 0]
            hi = hi + part_ref[a, 1]
    many = 8

    def group(g, _):
        accs = tuple(base_ref[pl.ds((g * many + k) * BLK, BLK), :] for k in range(many))

        def mode(n, accs):
            cr = coef_ref[n, 0]
            ci = coef_ref[n, 1]
            return tuple(
                accs[k]
                + (
                    cr * held[g * many + k, 0, pl.ds(n, 1), :]
                    + ci * held[g * many + k, 1, pl.ds(n, 1), :]
                )
                for k in range(many)
            )

        accs = lax.fori_loop(0, modes, mode, accs, unroll=4)
        for k in range(many):
            act_ref[pl.ds((g * many + k) * BLK, BLK), :] = jax.nn.gelu(accs[k]).astype(bf16)
        return 0

    lax.fori_loop(0, blocks // many, group, 0)


def params(limit=60):
    return pltpu.CompilerParams(vmem_limit_bytes=limit << 20)


def ends(signal, rates, freqs):
    tokens, channels = signal.shape
    modes = rates.shape[0]
    blocks = tokens // BLK
    pair = pl.BlockSpec((2, modes, LANES), lambda i: (0, 0, i))
    return pl.pallas_call(
        ends_kernel,
        grid=(channels // LANES,),
        in_specs=[
            pl.BlockSpec((tokens, LANES), lambda i: (0, i)),
            pl.BlockSpec((modes, LANES), lambda i: (0, i)),
            pl.BlockSpec((modes, LANES), lambda i: (0, i)),
        ],
        out_specs=[
            pl.BlockSpec((blocks, 2, modes, LANES), lambda i: (0, 0, 0, i)),
            pair,
            pair,
            pair,
            pl.BlockSpec((4, 2, modes, LANES), lambda i: (0, 0, 0, i)),
        ],
        out_shape=[
            jax.ShapeDtypeStruct((blocks, 2, modes, channels), f32),
            jax.ShapeDtypeStruct((2, modes, channels), f32),
            jax.ShapeDtypeStruct((2, modes, channels), bf16),
            jax.ShapeDtypeStruct((2, modes, channels), f32),
            jax.ShapeDtypeStruct((4, 2, modes, channels), f32),
        ],
        scratch_shapes=[
            pltpu.VMEM((tokens, LANES), f32),
            pltpu.VMEM((BLK, 2, modes, LANES), f32),
        ],
        compiler_params=params(),
        cost_estimate=pl.CostEstimate(flops=10**9, bytes_accessed=6 * 10**6, transcendentals=0),
    )(signal, rates, freqs)


def inner(first, count, signal, rates, freqs, coeffs, skip):
    tokens = signal.shape[0]
    modes = rates.shape[0]
    blocks = tokens // BLK
    return pl.pallas_call(
        inner_kernel,
        grid=(count,),
        in_specs=[
            pl.BlockSpec((tokens, LANES), lambda i: (0, i + first)),
            pl.BlockSpec((modes, LANES), lambda i: (0, i + first)),
            pl.BlockSpec((modes, LANES), lambda i: (0, i + first)),
            pl.BlockSpec((2, modes, LANES), lambda i: (0, 0, i + first)),
            pl.BlockSpec((1, LANES), lambda i: (0, i + first)),
        ],
        out_specs=[
            pl.BlockSpec((modes, 2, BLK, LANES), lambda i: (0, 0, 0, i)),
            pl.BlockSpec((tokens, LANES), lambda i: (0, i)),
        ],
        out_shape=[
            jax.ShapeDtypeStruct((modes, 2, BLK, count * LANES), f32),
            jax.ShapeDtypeStruct((tokens, count * LANES), f32),
        ],
        scratch_shapes=[
            pltpu.VMEM((blocks, BLK + 8, LANES), f32),
            pltpu.VMEM((10, modes, LANES), f32),
            pltpu.VMEM((BLK + 8, LANES), f32),
        ],
        compiler_params=params(14),
        cost_estimate=pl.CostEstimate(
            flops=10**8 * count, bytes_accessed=2 * 10**6 * count, transcendentals=0
        ),
    )(signal, rates, freqs, coeffs, skip)


def finish(first, count, part, step, coef, base, own, weight, arrived):
    blocks, _, modes, _ = part.shape
    tokens = base.shape[0]
    pair = pl.BlockSpec((2, modes, LANES), lambda i: (0, 0, i + first))
    return pl.pallas_call(
        finish_kernel,
        grid=(count,),
        in_specs=[
            pl.BlockSpec((blocks, 2, modes, LANES), lambda i: (0, 0, 0, i + first)),
            pair,
            pl.BlockSpec((modes, 2, BLK, LANES), lambda i: (0, 0, 0, i)),
            pl.BlockSpec((tokens, LANES), lambda i: (0, i)),
            pair,
            pair,
            pair,
        ],
        out_specs=pl.BlockSpec((tokens, LANES), lambda i: (0, i)),
        out_shape=jax.ShapeDtypeStruct((tokens, count * LANES), bf16),
        scratch_shapes=[pltpu.VMEM((blocks, 2, modes, LANES), f32)],
        compiler_params=params(14),
        cost_estimate=pl.CostEstimate(
            flops=10**9 // 6 * count, bytes_accessed=2 * 10**6 * count, transcendentals=0
        ),
    )(part, step, coef, base, own, weight, arrived)


def product_kernel(count, last, place_ref, *refs):
    acts = refs[:count]
    wide_ref = refs[count]
    more = refs[count + 1 : -1]
    out_ref = refs[-1]
    tile = out_ref.shape[1]
    depth = wide_ref.shape[0] // 4
    span = pl.ds(pl.multiple_of(pl.program_id(0) * tile, tile), tile)
    total = None
    for n, act in enumerate(acts):
        width = act.shape[1]
        start = place_ref[2 * n] * depth + place_ref[2 * n + 1] * width
        rows = pl.ds(pl.multiple_of(start, LANES), width)
        term = jnp.dot(act[...], wide_ref[rows, span], preferred_element_type=f32)
        total = term if total is None else total + term
    if last:
        total = total + more[0][:, span] + more[1][:, span].astype(f32)
    out_ref[...] = total.astype(out_ref.dtype)


def product(place, acts, wide, *more):
    tokens = acts[0].shape[0]
    channels = wide.shape[1]
    tile = 256
    inside = pl.BlockSpec(memory_space=pltpu.VMEM)
    last = bool(more)
    return pl.pallas_call(
        lambda *refs: product_kernel(len(acts), last, *refs),
        grid=(channels // tile,),
        in_specs=[pl.BlockSpec(memory_space=pltpu.SMEM)] + [inside] * (len(acts) + 1 + len(more)),
        out_specs=pl.BlockSpec((tokens, tile), lambda n: (0, n)),
        out_shape=jax.ShapeDtypeStruct((tokens, channels), bf16 if last else f32),
        compiler_params=params(12),
        cost_estimate=pl.CostEstimate(
            flops=4 * 10**8 * len(acts), bytes_accessed=10**6 * len(acts), transcendentals=0
        ),
    )(place, *acts, wide, *more)


def times(a, b):
    ar, ai = a[0].astype(f32), a[1].astype(f32)
    br, bi = b[0].astype(f32), b[1].astype(f32)
    return jnp.stack([ar * br - ai * bi, ar * bi + ai * br])


def partners(step):
    return [(i, i ^ step) for i in range(32)]


Y_STEP = [[(i, (i + k) % 4) for i in range(4)] for k in range(4)]


def after(value, *others):
    return lax.optimization_barrier((value, *others))[0]


def local(signal, rates, freqs, coeffs, skip, weight):
    index = lax.axis_index("seq")
    y = lax.axis_index("chan")
    skip = skip.reshape(1, -1)
    wide = lax.all_gather(weight, "seq", axis=0, tiled=True)
    part, end, send, step, powers = ends(signal, rates, freqs)

    mine = end
    scale = jnp.stack([jnp.ones_like(rates), jnp.zeros_like(rates)])
    own = jnp.zeros_like(end)
    inners = []
    for k in range(5):
        upper = (index >> k) % 2 == 1
        arrived = lax.ppermute(send, "seq", partners(1 << k))
        if k in (2, 3):
            s = k - 2
            inners.append(inner(3 * s, 3, after(signal, send), rates, freqs, coeffs, skip))
        if k == 4:
            scale = jnp.where(upper, scale, 0.0)
            break
        other = arrived.astype(f32)
        low = jnp.where(upper, other, mine)
        high = jnp.where(upper, mine, other)
        own = own + jnp.where(upper, times(scale, arrived), 0.0)
        scale = jnp.where(upper, times(scale, powers[k]), scale)
        mine = times(powers[k], low) + high
        send = mine.astype(bf16)

    acts, ups, downs, fars = [], [], [], []
    for s in range(2):
        act = finish(3 * s, 3, part, step, *inners[s], own, scale, arrived)
        up = lax.ppermute(act, "chan", Y_STEP[1])
        down = lax.ppermute(act, "chan", Y_STEP[3])
        fars.append(lax.ppermute(down if s else up, "chan", Y_STEP[3 if s else 1]))
        acts.append(act)
        ups.append(up)
        downs.append(down)
    mine, below, above, across = y, (y + 3) % 4, (y + 1) % 4, (y + 2) % 4
    zero = jnp.zeros_like(y)
    one = zero + 1
    first = jnp.stack([mine, zero, mine, one, below, zero, above, zero]).astype(jnp.int32)
    second = jnp.stack([below, one, above, one, across, zero, across, one]).astype(jnp.int32)
    total = product(first, [*acts, ups[0], downs[0]], wide)
    return product(second, [ups[1], downs[1], *fars], wide, total, signal)


def solution(mesh):
    in_specs = (
        P("seq", "chan"),
        P(None, "chan"),
        P(None, "chan"),
        P(None, None, "chan"),
        P("chan"),
        P("seq", "chan"),
    )
    return jax.shard_map(
        local, mesh=mesh, in_specs=in_specs, out_specs=P("seq", "chan"), check_vma=False
    )
```

```python
import jax
import jax.numpy as jnp
from jax import lax
from jax.experimental import pallas as pl
from jax.experimental.pallas import tpu as pltpu
from jax.sharding import PartitionSpec as P

BLK = 32
LANES = 128
GROUP = 4

f32 = jnp.float32
bf16 = jnp.bfloat16


def cmul(ar, ai, br, bi):
    return ar * br - ai * bi, ar * bi + ai * br


def decay(rates_ref, freqs_ref):
    size = jnp.exp(-rates_ref[...])
    angle = freqs_ref[...]
    return size * jnp.cos(angle), size * jnp.sin(angle)


def ends_kernel(u_ref, r_ref, f_ref, part_ref, end_ref, send_ref, step_ref, power_ref, uf, table):
    uf[...] = u_ref[...].astype(f32)
    lr, li = decay(r_ref, f_ref)
    powers = [(jnp.ones_like(lr), jnp.zeros_like(lr)), (lr, li)]
    for j in range(2, BLK + 1):
        half = powers[j // 2]
        powers.append(cmul(*half, *powers[j - j // 2]))
    for j in range(BLK):
        table[j, 0] = powers[j][0]
        table[j, 1] = powers[j][1]
    sr, si = powers[BLK]
    step_ref[0] = sr
    step_ref[1] = si
    wr, wi = sr, si
    count = BLK
    while count < u_ref.shape[0]:
        wr, wi = cmul(wr, wi, wr, wi)
        count *= 2
    for k in range(power_ref.shape[0]):
        power_ref[k, 0] = wr
        power_ref[k, 1] = wi
        wr, wi = cmul(wr, wi, wr, wi)

    def group(g, end):
        er, ei = end
        accs = [[jnp.zeros_like(lr), jnp.zeros_like(lr)] for _ in range(GROUP)]
        for b in range(BLK):
            tr = table[BLK - 1 - b, 0]
            ti = table[BLK - 1 - b, 1]
            for i in range(GROUP):
                row = uf[pl.ds((g * GROUP + i) * BLK + b, 1), :]
                accs[i][0] += tr * row
                accs[i][1] += ti * row
        for i in range(GROUP):
            part_ref[g * GROUP + i, 0] = accs[i][0]
            part_ref[g * GROUP + i, 1] = accs[i][1]
            er, ei = cmul(er, ei, sr, si)
            er = er + accs[i][0]
            ei = ei + accs[i][1]
        return er, ei

    er, ei = lax.fori_loop(
        0, u_ref.shape[0] // BLK // GROUP, group, (jnp.zeros_like(lr), jnp.zeros_like(lr))
    )
    end_ref[0] = er
    end_ref[1] = ei
    send_ref[0] = er.astype(bf16)
    send_ref[1] = ei.astype(bf16)


def inner_kernel(u_ref, r_ref, f_ref, c_ref, skip_ref, coef_ref, base_ref, pad, rows, taps):
    modes = r_ref.shape[0]
    lr, li = decay(r_ref, f_ref)
    q2 = cmul(lr, li, lr, li)
    q4 = cmul(*q2, *q2)
    q8 = cmul(*q4, *q4)
    cr = 2.0 * c_ref[0]
    ci = 2.0 * c_ref[1]
    first = cmul(cr, ci, lr, li)
    for k, pair in enumerate((first, (lr, li), q2, q4, q8)):
        rows[2 * k] = pair[0]
        rows[2 * k + 1] = pair[1]
    place = lax.broadcasted_iota(jnp.int32, (8, LANES), 0)
    bits = [(place & (1 << k)) != 0 for k in range(3)]

    def mode(n, sums):
        row = [jnp.broadcast_to(rows[k, pl.ds(n, 1), :], (8, LANES)) for k in range(10)]
        vr, vi = row[0], row[1]
        for k in range(3):
            nr, ni = cmul(vr, vi, row[2 + 2 * k], row[3 + 2 * k])
            vr = jnp.where(bits[k], nr, vr)
            vi = jnp.where(bits[k], ni, vi)
        out = []
        for i in range(BLK // 8):
            coef_ref[n, 0, 8 * i : 8 * i + 8] = vr
            coef_ref[n, 1, 8 * i : 8 * i + 8] = -vi
            out.append(sums[i] + vr)
            if i + 1 < BLK // 8:
                vr, vi = cmul(vr, vi, row[8], row[9])
        return tuple(out)

    zero = jnp.zeros((8, LANES), f32)
    sums = lax.fori_loop(0, modes, mode, (zero,) * (BLK // 8), unroll=8)
    taps[0:1] = jnp.sum(cr, axis=0, keepdims=True) + skip_ref[...]
    for i in range(BLK // 8):
        taps[8 * i + 1 : 8 * i + 9] = sums[i]
    blocks = u_ref.shape[0] // BLK
    pad[:, 0:8] = jnp.zeros((blocks, 8, LANES), f32)
    pad[:, 8:] = u_ref[...].astype(f32).reshape(blocks, BLK, LANES)

    def group(g, _):
        accs = [[zero] * (BLK // 8) for _ in range(GROUP)]
        for j in range(BLK):
            tap = jnp.broadcast_to(taps[j : j + 1], (8, LANES))
            for i in range(BLK // 8):
                if 8 * i + 7 >= j:
                    for k in range(GROUP):
                        accs[k][i] += tap * pad[g * GROUP + k, 8 + 8 * i - j : 16 + 8 * i - j]
        for k in range(GROUP):
            for i in range(BLK // 8):
                base_ref[pl.ds((g * GROUP + k) * BLK + 8 * i, 8), :] = accs[k][i]
        return 0

    lax.fori_loop(0, blocks // GROUP, group, 0)


def finish_kernel(part_ref, step_ref, coef_ref, base_ref, own_ref, w_ref, q_ref, act_ref, held):
    hr = own_ref[0]
    hi = own_ref[1]
    ar, ai = cmul(w_ref[0], w_ref[1], q_ref[0].astype(f32), q_ref[1].astype(f32))
    hr = hr + ar
    hi = hi + ai
    sr = step_ref[0]
    si = step_ref[1]
    blocks = part_ref.shape[0]
    modes = hr.shape[0]
    for a in range(blocks):
        held[a, 0] = hr
        held[a, 1] = hi
        if a + 1 < blocks:
            hr, hi = cmul(hr, hi, sr, si)
            hr = hr + part_ref[a, 0]
            hi = hi + part_ref[a, 1]
    many = 8

    def group(g, _):
        accs = tuple(base_ref[pl.ds((g * many + k) * BLK, BLK), :] for k in range(many))

        def mode(n, accs):
            cr = coef_ref[n, 0]
            ci = coef_ref[n, 1]
            return tuple(
                accs[k]
                + (
                    cr * held[g * many + k, 0, pl.ds(n, 1), :]
                    + ci * held[g * many + k, 1, pl.ds(n, 1), :]
                )
                for k in range(many)
            )

        accs = lax.fori_loop(0, modes, mode, accs, unroll=16)
        for k in range(many):
            act_ref[pl.ds((g * many + k) * BLK, BLK), :] = jax.nn.gelu(accs[k]).astype(bf16)
        return 0

    lax.fori_loop(0, blocks // many, group, 0)


def params(limit=60):
    return pltpu.CompilerParams(vmem_limit_bytes=limit << 20)


def ends(signal, rates, freqs):
    tokens, channels = signal.shape
    modes = rates.shape[0]
    blocks = tokens // BLK
    pair = pl.BlockSpec((2, modes, LANES), lambda i: (0, 0, i))
    return pl.pallas_call(
        ends_kernel,
        grid=(channels // LANES,),
        in_specs=[
            pl.BlockSpec((tokens, LANES), lambda i: (0, i)),
            pl.BlockSpec((modes, LANES), lambda i: (0, i)),
            pl.BlockSpec((modes, LANES), lambda i: (0, i)),
        ],
        out_specs=[
            pl.BlockSpec((blocks, 2, modes, LANES), lambda i: (0, 0, 0, i)),
            pair,
            pair,
            pair,
            pl.BlockSpec((4, 2, modes, LANES), lambda i: (0, 0, 0, i)),
        ],
        out_shape=[
            jax.ShapeDtypeStruct((blocks, 2, modes, channels), f32),
            jax.ShapeDtypeStruct((2, modes, channels), f32),
            jax.ShapeDtypeStruct((2, modes, channels), bf16),
            jax.ShapeDtypeStruct((2, modes, channels), f32),
            jax.ShapeDtypeStruct((4, 2, modes, channels), f32),
        ],
        scratch_shapes=[
            pltpu.VMEM((tokens, LANES), f32),
            pltpu.VMEM((BLK, 2, modes, LANES), f32),
        ],
        compiler_params=params(),
        cost_estimate=pl.CostEstimate(flops=10**9, bytes_accessed=6 * 10**6, transcendentals=0),
    )(signal, rates, freqs)


def inner(first, count, signal, rates, freqs, coeffs, skip):
    tokens = signal.shape[0]
    modes = rates.shape[0]
    blocks = tokens // BLK
    return pl.pallas_call(
        inner_kernel,
        grid=(count,),
        in_specs=[
            pl.BlockSpec((tokens, LANES), lambda i: (0, i + first)),
            pl.BlockSpec((modes, LANES), lambda i: (0, i + first)),
            pl.BlockSpec((modes, LANES), lambda i: (0, i + first)),
            pl.BlockSpec((2, modes, LANES), lambda i: (0, 0, i + first)),
            pl.BlockSpec((1, LANES), lambda i: (0, i + first)),
        ],
        out_specs=[
            pl.BlockSpec((modes, 2, BLK, LANES), lambda i: (0, 0, 0, i)),
            pl.BlockSpec((tokens, LANES), lambda i: (0, i)),
        ],
        out_shape=[
            jax.ShapeDtypeStruct((modes, 2, BLK, count * LANES), f32),
            jax.ShapeDtypeStruct((tokens, count * LANES), f32),
        ],
        scratch_shapes=[
            pltpu.VMEM((blocks, BLK + 8, LANES), f32),
            pltpu.VMEM((10, modes, LANES), f32),
            pltpu.VMEM((BLK + 8, LANES), f32),
        ],
        compiler_params=params(14),
        cost_estimate=pl.CostEstimate(
            flops=10**8 * count, bytes_accessed=2 * 10**6 * count, transcendentals=0
        ),
    )(signal, rates, freqs, coeffs, skip)


def finish(first, count, part, step, coef, base, own, weight, arrived):
    blocks, _, modes, _ = part.shape
    tokens = base.shape[0]
    pair = pl.BlockSpec((2, modes, LANES), lambda i: (0, 0, i + first))
    return pl.pallas_call(
        finish_kernel,
        grid=(count,),
        in_specs=[
            pl.BlockSpec((blocks, 2, modes, LANES), lambda i: (0, 0, 0, i + first)),
            pair,
            pl.BlockSpec((modes, 2, BLK, LANES), lambda i: (0, 0, 0, i)),
            pl.BlockSpec((tokens, LANES), lambda i: (0, i)),
            pair,
            pair,
            pair,
        ],
        out_specs=pl.BlockSpec((tokens, LANES), lambda i: (0, i)),
        out_shape=jax.ShapeDtypeStruct((tokens, count * LANES), bf16),
        scratch_shapes=[pltpu.VMEM((blocks, 2, modes, LANES), f32)],
        compiler_params=params(14),
        cost_estimate=pl.CostEstimate(
            flops=10**9 // 6 * count, bytes_accessed=2 * 10**6 * count, transcendentals=0
        ),
    )(part, step, coef, base, own, weight, arrived)


def product_kernel(count, last, place_ref, *refs):
    acts = refs[:count]
    wide_ref = refs[count]
    more = refs[count + 1 : -1]
    out_ref = refs[-1]
    tile = out_ref.shape[1]
    depth = wide_ref.shape[0] // 4
    span = pl.ds(pl.multiple_of(pl.program_id(0) * tile, tile), tile)
    total = None
    for n, act in enumerate(acts):
        width = act.shape[1]
        start = place_ref[2 * n] * depth + place_ref[2 * n + 1] * width
        rows = pl.ds(pl.multiple_of(start, LANES), width)
        term = jnp.dot(act[...], wide_ref[rows, span], preferred_element_type=f32)
        total = term if total is None else total + term
    if last:
        total = total + more[0][:, span] + more[1][:, span].astype(f32)
    out_ref[...] = total.astype(out_ref.dtype)


def product(place, acts, wide, *more):
    tokens = acts[0].shape[0]
    channels = wide.shape[1]
    tile = 256
    inside = pl.BlockSpec(memory_space=pltpu.VMEM)
    last = bool(more)
    return pl.pallas_call(
        lambda *refs: product_kernel(len(acts), last, *refs),
        grid=(channels // tile,),
        in_specs=[pl.BlockSpec(memory_space=pltpu.SMEM)] + [inside] * (len(acts) + 1 + len(more)),
        out_specs=pl.BlockSpec((tokens, tile), lambda n: (0, n)),
        out_shape=jax.ShapeDtypeStruct((tokens, channels), bf16 if last else f32),
        compiler_params=params(12),
        cost_estimate=pl.CostEstimate(
            flops=4 * 10**8 * len(acts), bytes_accessed=10**6 * len(acts), transcendentals=0
        ),
    )(place, *acts, wide, *more)


def times(a, b):
    ar, ai = a[0].astype(f32), a[1].astype(f32)
    br, bi = b[0].astype(f32), b[1].astype(f32)
    return jnp.stack([ar * br - ai * bi, ar * bi + ai * br])


def partners(step):
    return [(i, i ^ step) for i in range(32)]


Y_STEP = [[(i, (i + k) % 4) for i in range(4)] for k in range(4)]


def after(value, *others):
    return lax.optimization_barrier((value, *others))[0]


def local(signal, rates, freqs, coeffs, skip, weight):
    index = lax.axis_index("seq")
    y = lax.axis_index("chan")
    skip = skip.reshape(1, -1)
    wide = lax.all_gather(weight, "seq", axis=0, tiled=True)
    part, end, send, step, powers = ends(signal, rates, freqs)

    mine = end
    scale = jnp.stack([jnp.ones_like(rates), jnp.zeros_like(rates)])
    own = jnp.zeros_like(end)
    inners = []
    for k in range(5):
        upper = (index >> k) % 2 == 1
        arrived = lax.ppermute(send, "seq", partners(1 << k))
        if k in (2, 3):
            s = k - 2
            inners.append(inner(3 * s, 3, after(signal, send), rates, freqs, coeffs, skip))
        if k == 4:
            scale = jnp.where(upper, scale, 0.0)
            break
        other = arrived.astype(f32)
        low = jnp.where(upper, other, mine)
        high = jnp.where(upper, mine, other)
        own = own + jnp.where(upper, times(scale, arrived), 0.0)
        scale = jnp.where(upper, times(scale, powers[k]), scale)
        mine = times(powers[k], low) + high
        send = mine.astype(bf16)

    acts, ups, downs, fars = [], [], [], []
    for s in range(2):
        act = finish(3 * s, 3, part, step, *inners[s], own, scale, arrived)
        up = lax.ppermute(act, "chan", Y_STEP[1])
        down = lax.ppermute(act, "chan", Y_STEP[3])
        fars.append(lax.ppermute(down if s else up, "chan", Y_STEP[3 if s else 1]))
        acts.append(act)
        ups.append(up)
        downs.append(down)
    mine, below, above, across = y, (y + 3) % 4, (y + 1) % 4, (y + 2) % 4
    zero = jnp.zeros_like(y)
    one = zero + 1
    first = jnp.stack([mine, zero, mine, one, below, zero, above, zero]).astype(jnp.int32)
    second = jnp.stack([below, one, above, one, across, zero, across, one]).astype(jnp.int32)
    total = product(first, [*acts, ups[0], downs[0]], wide)
    return product(second, [ups[1], downs[1], *fars], wide, total, signal)


def solution(mesh):
    in_specs = (
        P("seq", "chan"),
        P(None, "chan"),
        P(None, "chan"),
        P(None, None, "chan"),
        P("chan"),
        P("seq", "chan"),
    )
    return jax.shard_map(
        local, mesh=mesh, in_specs=in_specs, out_specs=P("seq", "chan"), check_vma=False
    )
```
